32 devices in a mesh: pair: 8 (over z, x), virt: 4 (over y, core).
Axes of the slice: x: 2, y: 2, z: 4, core: 2. Of those that a mesh axis runs over, the one named last changes fastest.
Arguments:
- amps: bfloat16 [1792, 480, 480], P('pair', 'virt'), may hold values from -6 to 6
- integrals: bfloat16 [2304, 230400], P(None, ('virt', 'pair')), may hold values from -0.01171875 to 0.01171875
- slot_pair: int32 [1792], P('pair'), may hold values from -1 to 1175, as said below
- occ_energy: float32 [48], replicated, may hold values from -1.2 to -0.4
- virt_energy: float32 [48], replicated, may hold values from 0.3 to 1.5
Outputs:
- update: float32 [1792, 48, 48], P('pair', 'virt')
The draws below stay inside these ranges and needn't reach their ends.
Inputs may be any that keep to these rules, and one draw needn't show every extreme that they name: `slot_pair`: each of the 1176 pairs i <= j stands in exactly one slot, -1 marks an empty slot; the 224 slots of one index of pair hold uneven numbers of pairs, and some index has all 224 filled.
All inputs are finite; a program needn't handle non-finite values.
Results may differ from the reference program's by a relative error of at most 0.0003.
Values may be sent and summed in bfloat16 or wider, within the bound.
A program may use at most 192 MiB of HBM per device.

```python
import jax
import jax.numpy as jnp

NOCC = 48
NVIR = 480
WIN = 48
NPAIRS = 1176
SLOTS = 224
SLOTS_ALL = 1792
WW = 2304
CD = 230400
N_PAIR = 8


def draw_slot_pair(key, part):
    key_order, key_fullest, key_rest = jax.random.split(key, 3)
    shuffled = jax.random.permutation(key_order, NPAIRS).astype(jnp.int32)
    fullest = jax.random.randint(key_fullest, (), 0, N_PAIR).astype(jnp.int32)
    remaining = jax.random.permutation(key_rest, SLOTS_ALL - SLOTS)[:NPAIRS - SLOTS].astype(jnp.int32)
    positions = jnp.where(remaining < fullest * SLOTS, remaining, remaining + SLOTS)
    slots_out = jnp.full((SLOTS_ALL,), -1, jnp.int32)
    slots_out = slots_out.at[fullest * SLOTS + jnp.arange(SLOTS, dtype=jnp.int32)].set(shuffled[:SLOTS])
    slots_out = slots_out.at[positions].set(shuffled[SLOTS:])
    return slots_out


def block_scale(key, shape, shards, low, top_value):
    factor_of = 1.0
    for axis_at, parts in shards:
        heights = jax.random.uniform(jax.random.fold_in(jax.random.fold_in(key, 6), axis_at), (parts,), jnp.float32, low / len(shards), top_value / len(shards))
        factor_of = factor_of * jnp.repeat(jnp.exp(heights), shape[axis_at] // parts).reshape((-1,) + (1,) * (len(shape) - 1 - axis_at))
    return factor_of


def centred(rng, dims, scale, most, shards=(), kind=jnp.bfloat16):
    entries = scale * jax.random.normal(rng, dims, jnp.float32)
    if shards:
        entries = entries * block_scale(rng, dims, shards, -0.22, 0.18)
    return jnp.clip(entries, -most, most).astype(kind)


def setup_inputs(seed: int = 0) -> dict:
    arg_keys = jax.random.split(jax.random.key(seed), 6)
    amps = centred(arg_keys[0], (SLOTS_ALL, NVIR, NVIR), 1.0, 6.0, ((0, 8), (1, 4)))
    integrals = centred(arg_keys[1], (WW, CD), CD ** -0.5, 0.01171875, ((1, 32),))
    slot_pair = draw_slot_pair(jax.random.fold_in(arg_keys[5], 71), 0)
    occ_energy = jnp.clip(jax.random.uniform(arg_keys[3], (NOCC,), jnp.float32, -1.2, -0.4), -1.2, -0.4)
    virt_energy = jnp.clip(jax.random.uniform(arg_keys[4], (WIN,), jnp.float32, 0.3, 1.5), 0.3, 1.5)
    return {"amps": amps, "integrals": integrals, "slot_pair": slot_pair, "occ_energy": occ_energy, "virt_energy": virt_energy}


def pair_energy(slot_pair, occ_energy):
    nocc_count = occ_energy.shape[0]
    orbital = jnp.arange(nocc_count, dtype=jnp.int32)
    starts_row = orbital * nocc_count - orbital * (orbital - 1) // 2
    row_index = jnp.sum((starts_row[None, 1:] <= slot_pair[:, None]).astype(jnp.int32), axis=1)
    same_row = orbital[None, :] == row_index[:, None]
    row_start = jnp.sum(jnp.where(same_row, starts_row[None, :], 0), axis=1).astype(jnp.int32)
    column_index = slot_pair - row_start + row_index
    first_energy = jnp.sum(jnp.where(same_row, occ_energy[None, :], jnp.zeros_like(occ_energy)[None, :]), axis=1)
    same_column = orbital[None, :] == column_index[:, None]
    second_energy = jnp.sum(jnp.where(same_column, occ_energy[None, :], jnp.zeros_like(occ_energy)[None, :]), axis=1)
    return first_energy + second_energy, slot_pair >= 0


def reference(amps, integrals, slot_pair, occ_energy, virt_energy):
    count_all = amps.shape[0]
    window = virt_energy.shape[0]
    ladder = jnp.dot(amps.reshape(count_all, -1), integrals.T, preferred_element_type=jnp.float32)
    ladder = ladder.reshape(count_all, window, window)
    residual = ladder + jnp.transpose(ladder, (0, 2, 1))
    pair_sum, filled = pair_energy(slot_pair, occ_energy)
    denominator = pair_sum[:, None, None] - virt_energy[None, :, None] - virt_energy[None, None, :]
    return jnp.where(filled[:, None, None], residual / denominator, jnp.zeros_like(residual))
```

```python
import functools

import jax
import jax.numpy as jnp
from jax import lax
from jax.experimental import pallas as pl
from jax.experimental.pallas import tpu as pltpu
from jax.sharding import PartitionSpec as P


def pair_energy(slot_pair, occ_energy):
    nocc_count = occ_energy.shape[0]
    orbital = jnp.arange(nocc_count, dtype=jnp.int32)
    starts_row = orbital * nocc_count - orbital * (orbital - 1) // 2
    row_index = jnp.sum((starts_row[None, 1:] <= slot_pair[:, None]).astype(jnp.int32), axis=1)
    same_row = orbital[None, :] == row_index[:, None]
    row_start = jnp.sum(jnp.where(same_row, starts_row[None, :], 0), axis=1)
    column_index = slot_pair - row_start + row_index
    first_energy = jnp.sum(
        jnp.where(same_row, occ_energy[None, :], jnp.zeros_like(occ_energy)[None, :]), axis=1
    )
    same_column = orbital[None, :] == column_index[:, None]
    second_energy = jnp.sum(
        jnp.where(same_column, occ_energy[None, :], jnp.zeros_like(occ_energy)[None, :]), axis=1
    )
    return (first_energy + second_energy, slot_pair >= 0)


def ladder_term(row_block, columns):
    partial_value = lax.dot_general(
        row_block, columns, (((1,), (1,)), ((), ())), preferred_element_type=jnp.float32
    )
    return partial_value


def body(amps, integrals, slot_pair, occ_energy, virt_energy):
    slot_count = amps.shape[0]
    local_width = amps.shape[1] * amps.shape[2]
    flattened = amps.reshape(slot_count, local_width)
    window = virt_energy.shape[0]
    virt_count = lax.axis_size("virt")
    local_rows = window // virt_count
    panels = lax.all_to_all(flattened, "pair", split_axis=1, concat_axis=0, tiled=True)
    owned = lax.psum_scatter(
        ladder_term(panels, integrals), "pair", scatter_dimension=0, tiled=True
    )
    owned = lax.psum_scatter(
        owned.reshape(slot_count, window, window), "virt", scatter_dimension=1, tiled=True
    )
    flipped = lax.all_to_all(owned, "virt", split_axis=2, concat_axis=1, tiled=True)
    residual = owned + jnp.transpose(flipped, (0, 2, 1))
    pair_sum, filled = pair_energy(slot_pair, occ_energy)
    local_energy = lax.dynamic_slice_in_dim(
        virt_energy, lax.axis_index("virt") * local_rows, local_rows
    )
    denominator = pair_sum[:, None, None] - local_energy[None, :, None] - virt_energy[None, None, :]
    return jnp.where(filled[:, None, None], residual / denominator, jnp.zeros_like(residual))


ROWS = 32
TILE = 256
LANES = 128


def exchange_kernel(count, fold, window, send, integrals, update, landed, crossed, weights, panel,
                    stage, folded, arrived, total, turned, returned, send_sem, recv_sem, load_sem,
                    panel_sem, cross_send, cross_recv, arrived_sem, back_send, back_recv):
    me = lax.axis_index("pair")
    chunks = send.shape[0]
    halves = stage.shape[0]
    column = lax.axis_index("virt")
    local = window // fold
    barrier = pltpu.get_barrier_semaphore()
    for step in range(1, count):
        pl.semaphore_signal(
            barrier, inc=1, device_id={"pair": lax.rem(me + step, count)},
            device_id_type=pl.DeviceIdType.MESH,
        )
    for step in range(1, fold):
        pl.semaphore_signal(
            barrier, inc=1, device_id={"virt": lax.rem(column + step, fold)},
            device_id_type=pl.DeviceIdType.MESH,
        )
    pl.semaphore_wait(barrier, count + fold - 2)

    def remote(index, step):
        target = lax.rem(me + step, count)
        return pltpu.make_async_remote_copy(
            src_ref=send.at[index, target],
            dst_ref=landed.at[index, pl.ds(pl.multiple_of(me * ROWS, ROWS), ROWS)],
            send_sem=send_sem.at[index, step - 1],
            recv_sem=recv_sem.at[index, step - 1],
            device_id={"pair": target},
            device_id_type=pl.DeviceIdType.MESH,
        )

    def start(index):
        for step in range(1, count):
            remote(index, step).start()

    def landing(index, step):
        origin = lax.rem(me + count - step, count)
        return pltpu.make_async_remote_copy(
            src_ref=send.at[index, origin],
            dst_ref=landed.at[index, pl.ds(pl.multiple_of(origin * ROWS, ROWS), ROWS)],
            send_sem=send_sem.at[index, step - 1],
            recv_sem=recv_sem.at[index, step - 1],
            device_id={"pair": origin},
            device_id_type=pl.DeviceIdType.MESH,
        )

    def across(index, step):
        target = lax.rem(column + step, fold)
        return pltpu.make_async_remote_copy(
            src_ref=folded.at[pl.ds(target * local, local)],
            dst_ref=crossed.at[index, step - 1],
            send_sem=cross_send.at[index, step - 1],
            recv_sem=cross_recv.at[index, step - 1],
            device_id={"virt": target},
            device_id_type=pl.DeviceIdType.MESH,
        )

    def back(index, step):
        target = lax.rem(me + step, count)
        return pltpu.make_async_remote_copy(
            src_ref=turned.at[pl.ds(pl.multiple_of(target * ROWS, ROWS), ROWS)],
            dst_ref=returned.at[step, pl.ds(pl.multiple_of(index * ROWS, ROWS), ROWS)],
            send_sem=back_send.at[index, step - 1],
            recv_sem=back_recv.at[index, step - 1],
            device_id={"pair": target},
            device_id_type=pl.DeviceIdType.MESH,
        )

    total[...] = jnp.zeros_like(total)
    start(0)
    if chunks > 1:
        start(1)
    load = pltpu.make_async_copy(integrals, weights, load_sem)
    load.start()
    load.wait()

    def one(index, carry):
        for step in range(1, count):
            landing(index, step).wait_recv()

        @pl.when(index + 2 < chunks)
        def _():
            start(index + 2)

        for step in range(count):
            origin = lax.rem(me + count - step, count)
            place = pl.ds(pl.multiple_of(origin * ROWS, ROWS), ROWS)
            source = send.at[index, origin] if step == 0 else landed.at[index, place]
            pltpu.make_async_copy(source, panel.at[place], panel_sem.at[step]).start()
        for step in range(count):
            origin = lax.rem(me + count - step, count)
            place = pl.ds(pl.multiple_of(origin * ROWS, ROWS), ROWS)
            source = send.at[index, origin] if step == 0 else landed.at[index, place]
            pltpu.make_async_copy(source, panel.at[place], panel_sem.at[step]).wait()

        def columns(tile, inner):
            place = pl.ds(pl.multiple_of(tile * TILE, TILE), TILE)
            term = jnp.dot(panel[...], weights[:, place], preferred_element_type=jnp.float32)
            for half in range(halves):
                stage[half, place, :] = term[half * LANES:(half + 1) * LANES].T
            return inner

        lax.fori_loop(0, stage.shape[1] // TILE, columns, 0)
        for row in range(window):
            for half in range(halves):
                folded[row, :, half * LANES:(half + 1) * LANES] = (
                    stage[half, row * window:(row + 1) * window, :]
                    + stage[half, pl.ds(row, window, stride=window), :]
                )
        for step in range(1, fold):
            across(index, step).start()
        for step in range(1, fold):
            across(index, step).wait_recv()
        for step in range(1, fold):
            pltpu.make_async_copy(
                crossed.at[index, step - 1], arrived.at[step - 1], arrived_sem.at[step - 1]
            ).start()
        for step in range(1, fold):
            pltpu.make_async_copy(
                crossed.at[index, step - 1], arrived.at[step - 1], arrived_sem.at[step - 1]
            ).wait()
        for row in range(local):
            value = folded[column * local + row]
            for step in range(1, fold):
                value = value + arrived[step - 1, row]
            total[row * window:(row + 1) * window, :] = value

        @pl.when(index > 0)
        def _():
            for step in range(1, count):
                back(index - 1, step).wait_send()

        for part in range(turned.shape[1] // LANES):
            turned[:, part * LANES:(part + 1) * LANES] = total[part * LANES:(part + 1) * LANES, :].T
        for step in range(1, count):
            back(index, step).start()
        mine = pl.ds(pl.multiple_of(me * ROWS, ROWS), ROWS)
        returned[0, pl.ds(pl.multiple_of(index * ROWS, ROWS), ROWS), :] = turned[mine, :]
        for step in range(1, fold):
            across(index, step).wait_send()
        for step in range(1, count):
            remote(index, step).wait_send()
        return carry

    lax.fori_loop(0, chunks, one, 0)
    for step in range(1, count):
        back(chunks - 1, step).wait_send()

    def gather(index, carry):
        for step in range(1, count):
            back(index, step).wait_recv()
        place = pl.ds(pl.multiple_of(index * ROWS, ROWS), ROWS)
        value = returned[0, place, :]
        for step in range(1, count):
            value = value + returned[step, place, :]
        update[place, :] = value
        return carry

    lax.fori_loop(0, chunks, gather, 0)


def exchanged_ladder(send, weights, window):
    chunks, count, rows, width = send.shape
    lanes = count * rows
    fold = lax.axis_size("virt")
    local = window // fold
    padded = -(-local * window // LANES) * LANES
    call = pl.pallas_call(
        functools.partial(exchange_kernel, count, fold, window),
        out_shape=(
            jax.ShapeDtypeStruct((chunks * rows, padded), jnp.float32),
            jax.ShapeDtypeStruct((chunks, lanes, width), send.dtype),
            jax.ShapeDtypeStruct((chunks, fold - 1, local, window, lanes), jnp.float32),
        ),
        in_specs=[pl.BlockSpec(memory_space=pl.ANY)] * 2,
        out_specs=(pl.BlockSpec(memory_space=pltpu.VMEM),) + (pl.BlockSpec(memory_space=pl.ANY),) * 2,
        scratch_shapes=[
            pltpu.VMEM(weights.shape, weights.dtype),
            pltpu.VMEM((lanes, width), send.dtype),
            pltpu.VMEM((lanes // LANES, window * window, LANES), jnp.float32),
            pltpu.VMEM((window, window, lanes), jnp.float32),
            pltpu.VMEM((fold - 1, local, window, lanes), jnp.float32),
            pltpu.VMEM((padded, lanes), jnp.float32),
            pltpu.VMEM((lanes, padded), jnp.float32),
            pltpu.VMEM((count, chunks * rows, padded), jnp.float32),
            pltpu.SemaphoreType.DMA((chunks, count - 1)),
            pltpu.SemaphoreType.DMA((chunks, count - 1)),
            pltpu.SemaphoreType.DMA(()),
            pltpu.SemaphoreType.DMA((count,)),
            pltpu.SemaphoreType.DMA((chunks, fold - 1)),
            pltpu.SemaphoreType.DMA((chunks, fold - 1)),
            pltpu.SemaphoreType.DMA((fold - 1,)),
            pltpu.SemaphoreType.DMA((chunks, count - 1)),
            pltpu.SemaphoreType.DMA((chunks, count - 1)),
        ],
        compiler_params=pltpu.CompilerParams(
            collective_id=1, has_side_effects=True, vmem_limit_bytes=58 * 2**20
        ),
        cost_estimate=pl.CostEstimate(
            flops=2 * chunks * lanes * width * window * window,
            bytes_accessed=2 * (weights.size + 3 * send.size), transcendentals=0,
        ),
    )
    return call(send, weights)[0][:, :local * window]


def overlapped_body(amps, integrals, slot_pair, occ_energy, virt_energy):
    slot_count = amps.shape[0]
    window = virt_energy.shape[0]
    pair_count = lax.axis_size("pair")
    virt_count = lax.axis_size("virt")
    local_rows = window // virt_count
    width = amps.shape[1] * amps.shape[2] // pair_count
    groups = slot_count // ROWS
    send = amps.reshape(groups, ROWS, pair_count, width).transpose(0, 2, 1, 3)
    weights = integrals.T
    residual = exchanged_ladder(send, weights, window)
    residual = residual.reshape(slot_count, local_rows, window).transpose(1, 2, 0)
    pair_sum, filled = pair_energy(slot_pair, occ_energy)
    local_energy = lax.dynamic_slice_in_dim(
        virt_energy, lax.axis_index("virt") * local_rows, local_rows
    )
    denominator = pair_sum[None, None, :] - local_energy[:, None, None] - virt_energy[None, :, None]
    update = jnp.where(filled[None, None, :], residual / denominator, jnp.zeros_like(residual))
    return jnp.transpose(update, (2, 0, 1))


def chosen_body(amps, *rest):
    slot_count = amps.shape[0]
    window = rest[-1].shape[0]
    lanes = lax.axis_size("pair") * ROWS
    fits = (
        slot_count % ROWS == 0 and slot_count // ROWS > 1 and lanes == 2 * LANES
        and window * window % TILE == 0
    )
    return (overlapped_body if fits else body)(amps, *rest)


def solution(mesh):
    placed = (P("pair", "virt", None), P(None, ("virt", "pair")), P("pair"), P(), P())
    return jax.shard_map(
        chosen_body, mesh=mesh, in_specs=placed, out_specs=P("pair", "virt", None), check_vma=False
    )
```
